256 devices in a mesh: dp: 32 (over y, z_hi, x), mp: 8 (over z_lo, core).
Axes of the slice: x: 4, y: 4, z: 8 (z_hi: 2, z_lo: 4; z = z_hi * 4 + z_lo), core: 2. Of those that a mesh axis runs over, the one named last changes fastest.
Arguments:
- acts: bfloat16 [1, 131072, 8192], P(None, 'dp', 'mp'), may hold values from -6 to 6
- rank_space_gradient: bfloat16 [1, 131072, 16], P(None, 'dp'), may hold values from -0.15625 to 0.15625
- running_factor_blocks: float32 [8, 1024, 1024], P('mp', 'dp')
- inverse_root_blocks: float32 [8, 1024, 1024], P('mp', 'dp')
- owner_block_order: int32 [8], replicated, may hold values from 0 to 7, each once
- refresh: int32 [8], replicated, may hold values 0 or 1
Outputs:
- factor_new: float32 [8, 1024, 1024], P('mp', 'dp')
- roots_new: float32 [8, 1024, 1024], P('mp', 'dp')
- update: float32 [1, 16, 8192], replicated
The draws below stay inside these ranges and needn't reach their ends.
Inputs may be any that keep to these rules, and one draw needn't show every extreme that they name: `owner_block_order`: a permutation: every block appears at exactly one owner position.
All inputs are finite; a program needn't handle non-finite values.
Results may differ from the reference program's by a relative error of at most 0.0003.
Values sent between devices are 32-bit elements; how exact they have to be, the bound alone decides.
A program may use at most 64 MiB of HBM per device.

```python
import math
import jax
import jax.numpy as jnp
from jax import lax

D = 8192
BS = 1024
ADAPTER_RANK = 16
LAYER_TOTAL = 1
TOKEN_TOTAL = 131072
NBLK = 8


def symmetric_noise(key, coefficient):
    base = jax.random.normal(key, (NBLK, BS, BS), jnp.float32)
    return (base + jnp.swapaxes(base, 1, 2)) * (coefficient / math.sqrt(BS))


def draw_running_factor_blocks(key, part):
    key = jax.random.fold_in(key, 11)
    diag_key, noise_key = jax.random.split(key)
    levels = jnp.exp(jax.random.uniform(diag_key, (NBLK, BS), jnp.float32, math.log(0.5), math.log(2.0)))
    eye_block = jnp.eye(BS, dtype=jnp.float32)
    return levels[:, :, None] * eye_block[None] + symmetric_noise(noise_key, 0.15)


def draw_inverse_root_blocks(key, part):
    key = jax.random.fold_in(key, 23)
    diag_key, noise_key = jax.random.split(key)
    levels = 0.8 * jax.random.uniform(diag_key, (NBLK, BS), jnp.float32, 0.85, 1.15)
    eye_block = jnp.eye(BS, dtype=jnp.float32)
    return levels[:, :, None] * eye_block[None] + symmetric_noise(noise_key, 0.12)


def with_ends(array, key, smallest, high):
    dims = array.shape
    index_at = [jax.random.randint(jax.random.fold_in(key, axis), (), 0, dims[axis]) for axis in range(len(dims))]
    array = array.at[tuple(index_at)].set(smallest)
    longest = dims.index(max(dims))
    index_at[longest] = (index_at[longest] + 1) % dims[longest]
    return array.at[tuple(index_at)].set(high)


def block_scale(rng, dims, pieces, low, top_value):
    def one(dim, shards_of):
        draws = jax.random.uniform(jax.random.fold_in(jax.random.fold_in(rng, 6), dim), (shards_of,), jnp.float32, low / len(pieces), top_value / len(pieces))
        return jnp.repeat(jnp.exp(draws), dims[dim] // shards_of).reshape((-1,) + (1,) * (len(dims) - dim - 1))

    gain = one(*pieces[0])
    for cut in pieces[1:]:
        gain = gain * one(*cut)
    return gain


def centred(stream_key, extent, spread, most, cuts=(), kind=jnp.bfloat16):
    array = jax.random.normal(stream_key, extent, jnp.float32) * spread
    if len(cuts) > 0:
        array = block_scale(stream_key, extent, cuts, -0.22, 0.18) * array
    return jnp.clip(array, min=-most, max=most).astype(kind)


def setup_inputs(seed: int = 0) -> dict:
    splits = jax.random.split(jax.random.key(seed), 7)
    acts = centred(splits[0], (LAYER_TOTAL, TOKEN_TOTAL, D), 1.0, 6.0, ((1, 32), (2, 8)))
    rank_space_gradient = centred(splits[1], (LAYER_TOTAL, TOKEN_TOTAL, ADAPTER_RANK), 0.011, 0.15625, ((1, 32),))
    running_factor_blocks = draw_running_factor_blocks(jax.random.fold_in(splits[6], 71), 0)
    inverse_root_blocks = draw_inverse_root_blocks(jax.random.fold_in(splits[6], 71), 0)
    owner_block_order = jax.random.permutation(splits[4], NBLK).astype(jnp.int32)
    refresh = with_ends((jax.random.randint(splits[5], (NBLK,), 0, 2) < 1).astype(jnp.int32), jax.random.fold_in(splits[5], 1), 0, 1)
    return {"acts": acts, "rank_space_gradient": rank_space_gradient, "running_factor_blocks": running_factor_blocks, "inverse_root_blocks": inverse_root_blocks, "owner_block_order": owner_block_order, "refresh": refresh}


DECAY = 0.75
DAMPING = 0.1
HIGH = lax.Precision.HIGHEST


def reference(acts, rank_space_gradient, running_factor_blocks, inverse_root_blocks, owner_block_order, refresh):
    per_layer = D // BS
    eye_block = jnp.eye(BS, dtype=jnp.float32)

    def one_slot(inputs):
        position, old_factor, old_root = inputs
        block_id = owner_block_order[position]
        layer_number = block_id // per_layer
        offset = (block_id % per_layer) * BS
        columns = lax.dynamic_slice(acts, (layer_number, jnp.int32(0), offset), (1, TOKEN_TOTAL, BS))[0]
        incoming_signal = lax.dynamic_slice(rank_space_gradient, (layer_number, jnp.int32(0), jnp.int32(0)), (1, TOKEN_TOTAL, ADAPTER_RANK))[0]
        covariance = jnp.dot(columns.T, columns, preferred_element_type=jnp.float32) / TOKEN_TOTAL
        factor_next = DECAY * old_factor + (1.0 - DECAY) * covariance
        damped = factor_next + DAMPING * eye_block
        first_term = jnp.dot(old_root, damped, precision=HIGH, preferred_element_type=jnp.float32)
        second_term = jnp.dot(first_term, old_root, precision=HIGH, preferred_element_type=jnp.float32)
        third_term = jnp.dot(second_term, old_root, precision=HIGH, preferred_element_type=jnp.float32)
        stepped = 1.5 * old_root - 0.5 * third_term
        root_next = jnp.where(refresh[block_id] == 1, stepped, old_root)
        gradient = jnp.dot(columns.T, incoming_signal, preferred_element_type=jnp.float32)
        conditioned = jnp.dot(old_root, gradient, precision=HIGH, preferred_element_type=jnp.float32)
        return factor_next, root_next, conditioned

    positions = jnp.arange(NBLK, dtype=jnp.int32)
    factor_new, roots_new, conditioned = lax.map(one_slot, (positions, running_factor_blocks, inverse_root_blocks))
    ordered = jnp.zeros_like(conditioned).at[owner_block_order].set(conditioned)
    update = ordered.reshape(LAYER_TOTAL, per_layer, BS, ADAPTER_RANK).transpose(0, 3, 1, 2).reshape(LAYER_TOTAL, ADAPTER_RANK, D)
    return factor_new, roots_new, update
```

```python
import functools

import jax
import jax.numpy as jnp
from jax import lax
from jax.experimental import pallas as pl
from jax.experimental.pallas import tpu as pltpu
from jax.sharding import PartitionSpec as P

D = 8192
DECAY = 0.75
DAMPING = 0.1
MESH = pl.DeviceIdType.MESH
NN = (((1,), (0,)), ((), ()))
NT = (((1,), (1,)), ((), ()))
TN = (((0,), (0,)), ((), ()))
SEMS = 192
F32 = jnp.float32
BF16 = jnp.bfloat16

GROUPS = ((4, 5, 6, 7), (0, 1, 2, 3))


def width(p):
    return 640 if p <= 4 else 512


def dot(a, b, dims=NN):
    return lax.dot_general(a, b, dims, preferred_element_type=F32)


def split(v):
    high = v.astype(BF16)
    return high, (v - high.astype(F32)).astype(BF16)


def dot_split(stacked, high, low, dims=NN):
    rows = stacked.shape[0] // 2
    both = dot(stacked, high, dims)
    return both[:rows] + both[rows:] + dot(stacked[:rows], low, dims)


def kernel(
    tokens,
    order, refresh, x_hbm, g_hbm, r_hbm, y_hbm,
    fo, ro, uo,
    x, g, rsh, yb, yh, yl, ystk, pan, r1, s1, r2, zb0, zb1, sibs, sibr, cag,
    rcol, vs, vr, f, tb, ub, lsem, ssem, rsem,
):
    scale = (1.0 - DECAY) / tokens
    zb = (zb0, zb1)
    dp = lax.axis_index("dp")
    mp = lax.axis_index("mp")
    cy, czh, cx = dp // 8, (dp // 4) % 2, dp % 4
    czl, cc = mp // 2, mp % 2
    cz = czh * 4 + czl

    def dev(y, zh, xx, zl, c):
        return {"dp": (y * 2 + zh) * 4 + xx, "mp": zl * 2 + c}

    def zdev(d):
        w = (cz + d) % 8
        return dev(cy, w // 4, cx, w % 4, cc)

    px = {d: dev(cy, czh, (cx + d) % 4, czl, cc) for d in (1, 2, 3)}
    py = {d: dev((cy + d) % 4, czh, cx, czl, cc) for d in (1, 2, 3)}
    pa = {
        (dz, dx): dev(cy, (czh + dz) % 2, (cx + dx) % 4, czl, cc)
        for dz in (0, 1) for dx in (0, 1, 2, 3) if dz or dx
    }
    z_up, z_down = zdev(1), zdev(7)
    sibling = dev(cy, czh, cx, czl, 1 - cc)
    AX = {"x": (cx, px), "y": (cy, py)}

    count = [0]
    sent = []

    def send(src, dst, target):
        i = count[0]
        count[0] += 1
        copy = pltpu.make_async_remote_copy(
            src_ref=src, dst_ref=dst, send_sem=ssem.at[i], recv_sem=rsem.at[i],
            device_id=target, device_id_type=MESH,
        )
        copy.start()
        sent.append(copy)
        return copy

    def arrive(copies):
        for c in copies:
            c.wait_recv()

    own_y = yb.at[cy, czh, cx]
    load_y = pltpu.make_async_copy(y_hbm.at[0], own_y, lsem.at[0])
    load_r = pltpu.make_async_copy(r_hbm.at[0], rsh, lsem.at[1])
    load_y.start()
    load_r.start()
    nk = 4
    depth = x.shape[0] // nk
    load_x = [
        pltpu.make_async_copy(x_hbm.at[0, pl.ds(i * depth, depth)], x.at[pl.ds(i * depth, depth)], lsem.at[3 + i])
        for i in range(nk)
    ]
    for c in load_x:
        c.start()
    load_g = pltpu.make_async_copy(g_hbm, g, lsem.at[2])
    load_g.start()

    barrier = pltpu.get_barrier_semaphore()
    peers = list(pa.values()) + list(py.values()) + [z_up, z_down, sibling]
    for peer in peers:
        pl.semaphore_signal(barrier, inc=1, device_id=peer, device_id_type=MESH)
    pl.semaphore_wait(barrier, len(peers))

    def y_first(h):
        a = [send(yb.at[cy, h, cx, pl.ds(0, 16)], yb.at[cy, h, cx, pl.ds(0, 16)], px[d]) for d in (1, 2, 3)]
        b = [send(yb.at[cy, h, cx, pl.ds(16, 16)], yb.at[cy, h, cx, pl.ds(16, 16)], py[d]) for d in (1, 2, 3)]
        return a + b

    def y_second(h):
        a = [send(yb.at[cy, h, :, pl.ds(0, 16)], yb.at[cy, h, :, pl.ds(0, 16)], py[d]) for d in (1, 2, 3)]
        b = [send(yb.at[:, h, cx, pl.ds(16, 16)], yb.at[:, h, cx, pl.ds(16, 16)], px[d]) for d in (1, 2, 3)]
        return a + b

    my_j = czh * 4 + cx
    load_y.wait()
    y_z = send(own_y, own_y, pa[(1, 0)])
    y_own1 = y_first(czh)
    load_r.wait()
    r_a2a = []
    for (dz, dx), peer in pa.items():
        j = ((czh + dz) % 2) * 4 + (cx + dx) % 4
        r_a2a.append(
            send(rsh.at[:, pl.ds(pl.multiple_of(j * 128, 128), 128)], rcol.at[cy, my_j], peer)
        )
    rcol[cy, my_j] = rsh[:, pl.ds(pl.multiple_of(my_j * 128, 128), 128)]

    yr = yb[cy, czh, cx]
    yrh, yrl = split(yr)
    ystk[0:32, 0:1024] = yrh
    ystk[0:32, 1024:1536] = yrh[:, :512]
    ystk[32:64, 0:1024] = yrl
    ystk[32:64, 1024:1536] = yrl[:, :512]

    def gemm(i, k0, kn, first):
        lo = 256 * i
        n = 768 if i < 2 else 640
        segs = [(lo, n, 0)] if lo + n <= 1024 else [(lo, 1024 - lo, 0), (0, lo + n - 1024, 1024 - lo)]
        for start, w, at in segs:
            v = dot(x[k0:k0 + kn, lo:lo + 256], x[k0:k0 + kn, start:start + w], TN)
            for half in (0, 1):
                p = 2 * i + half
                cols = 640 if p < 4 else 512
                b0, b1 = max(at, 128 * half), min(at + w, 128 * half + cols)
                if b1 <= b0:
                    continue
                part = v[128 * half:128 * half + 128, b0 - at:b1 - at]
                c0 = b0 - 128 * half
                if first:
                    pan[p, :, c0:c0 + b1 - b0] = part
                else:
                    pan[p, :, c0:c0 + b1 - b0] += part

    ax1 = {p: AX["x" if p % 2 == 0 else "y"] for p in range(8)}
    ax2 = {p: AX["y" if p % 2 == 0 else "x"] for p in range(8)}

    def rs_first(p):
        a, peer = ax1[p]
        w = width(p)
        return [
            send(
                pan.at[p, pl.ds(pl.multiple_of(((a + d) % 4) * 32, 32), 32), pl.ds(0, w)],
                r1.at[p, d - 1, :, pl.ds(0, w)], peer[d],
            )
            for d in (1, 2, 3)
        ]

    def rs_second(p, copies):
        arrive(copies)
        a, _ = ax1[p]
        b, peer = ax2[p]
        w = width(p)
        s1[p, :, :w] = (
            pan[p, pl.ds(pl.multiple_of(a * 32, 32), 32), :w] + r1[p, 0, :, :w] + r1[p, 1, :, :w] + r1[p, 2, :, :w]
        )
        return [
            send(
                s1.at[p, pl.ds(pl.multiple_of(((b + d) % 4) * 8, 8), 8), pl.ds(0, w)],
                r2.at[p, d - 1, :, pl.ds(0, w)], peer[d],
            )
            for d in (1, 2, 3)
        ]

    def rs_end(p, copies):
        arrive(copies)
        b, _ = ax2[p]
        w = width(p)
        gi = 0 if p >= 4 else 1
        i = p % 4
        zb[gi][cz, 8 * i:8 * i + 8, :w] = (
            s1[p, pl.ds(pl.multiple_of(b * 8, 8), 8), :w] + r2[p, 0, :, :w] + r2[p, 1, :, :w] + r2[p, 2, :, :w]
        )
        if w < 640:
            zb[gi][cz, 8 * i:8 * i + 8, w:640] = jnp.zeros((8, 640 - w), F32)

    def z_step(gi, s):
        up, down = (cz - s) % 8, (cz + s) % 8
        if s < 3:
            u, v = zb[gi].at[up], zb[gi].at[down]
        else:
            u, v = zb[gi].at[up, pl.ds(0, 16)], zb[gi].at[down, pl.ds(16, 16)]
        return [send(u, u, z_up), send(v, v, z_down)]

    b_mine = order[2 * czl + cc]
    b_other = order[2 * czl + 1 - cc]

    def picked(gi, b):
        return zb[gi][b // 2] + zb[gi][b // 2 + 4]

    def to_sibling(gi):
        sibs[gi] = jnp.where(b_other % 2 == cc, picked(gi, b_other), 0.0)
        return [send(sibs.at[gi], sibr.at[gi], sibling)]

    def take(gi):
        v = jnp.where(b_mine % 2 == cc, picked(gi, b_mine), sibr[gi])
        for i, p in enumerate(GROUPS[gi]):
            a, _ = ax1[p]
            b, _ = ax2[p]
            w = width(p)
            cag[p, pl.ds(pl.multiple_of(a * 32 + b * 8, 8), 8), :w] = v[8 * i:8 * i + 8, :w]

    def ag_first(p):
        a, _ = ax1[p]
        b, peer = ax2[p]
        ref = cag.at[p, pl.ds(pl.multiple_of(a * 32 + b * 8, 8), 8), pl.ds(0, width(p))]
        return [send(ref, ref, peer[d]) for d in (1, 2, 3)]

    def ag_second(p, copies):
        arrive(copies)
        a, peer = ax1[p]
        ref = cag.at[p, pl.ds(pl.multiple_of(a * 32, 32), 32), pl.ds(0, width(p))]
        return [send(ref, ref, peer[d]) for d in (1, 2, 3)]

    c1, c2 = {}, {}
    for k in range(nk):
        load_x[k].wait()
        gemm(2, k * depth, depth, k == 0)
    load_g.wait()
    grads = dot(g[...], x[...])
    for j in range(8):
        pan[4, 16 * j:16 * j + 16, 512:640] = grads[:, 128 * j:128 * j + 128]
    c1[4], c1[5] = rs_first(4), rs_first(5)
    y_z.wait_recv()
    y_oth1 = y_first(1 - czh)
    gemm(3, 0, x.shape[0], True)
    c1[6], c1[7] = rs_first(6), rs_first(7)
    c2[4], c2[5] = rs_second(4, c1[4]), rs_second(5, c1[5])
    arrive(r_a2a)
    r_y = [send(rcol.at[cy], rcol.at[cy], py[d]) for d in (1, 2, 3)]
    gemm(0, 0, x.shape[0], True)
    c1[0], c1[1] = rs_first(0), rs_first(1)
    c2[6], c2[7] = rs_second(6, c1[6]), rs_second(7, c1[7])
    gemm(1, 0, x.shape[0], True)
    c1[2], c1[3] = rs_first(2), rs_first(3)
    arrive(y_own1)
    y_own2 = y_second(czh)
    c2[0], c2[1] = rs_second(0, c1[0]), rs_second(1, c1[1])
    for p in GROUPS[0]:
        rs_end(p, c2[p])
    za = z_step(0, 0)
    c2[2], c2[3] = rs_second(2, c1[2]), rs_second(3, c1[3])
    arrive(y_oth1)
    y_oth2 = y_second(1 - czh)
    for p in GROUPS[1]:
        rs_end(p, c2[p])
    zc = z_step(1, 0)
    for s in (1, 2, 3):
        arrive(za)
        za = z_step(0, s)
        arrive(zc)
        zc = z_step(1, s)
    arrive(za)
    sa = to_sibling(0)
    arrive(zc)
    sb = to_sibling(1)
    arrive(sa)
    take(0)
    g1 = {p: ag_first(p) for p in GROUPS[0]}
    arrive(sb)
    take(1)
    g1.update({p: ag_first(p) for p in GROUPS[1]})
    g2 = {p: ag_second(p, g1[p]) for p in GROUPS[0] + GROUPS[1]}

    arrive(y_own2)
    arrive(y_oth2)

    def convert(i, carry):
        v = yb[i // 8, (i // 4) % 2, i % 4]
        h, l = split(v)
        at = pl.ds(pl.multiple_of(i * 32, 32), 32)
        yh[at] = h
        yl[at] = l
        return carry

    lax.fori_loop(0, 32, convert, 0)
    arrive(r_y)
    n = 1024
    eye = (
        lax.broadcasted_iota(jnp.int32, (n, 128), 0) == lax.broadcasted_iota(jnp.int32, (n, 128), 1) + my_j * 128
    )
    rh, rl = split(DECAY * rcol[...].reshape(n, 128) + jnp.where(eye, DAMPING, 0.0))
    rows_i = pl.ds(pl.multiple_of(cy * 256, 256), 256)
    v = dot(yh[rows_i], rh) + dot(yl[rows_i], rh) + dot(yh[rows_i], rl)
    vs[...] = v.reshape(8, 32, 128)
    v_a2a = []
    for (dz, dx), peer in pa.items():
        j = ((czh + dz) % 2) * 4 + (cx + dx) % 4
        v_a2a.append(send(vs.at[j], vr.at[my_j], peer))
    vr[my_j] = vs[my_j]

    arrive(g2[4])
    pr = pl.ds(pl.multiple_of((2 * cy + czh) * 128, 128), 128)
    gk = jnp.concatenate([cag[4, 16 * j:16 * j + 16, 512:640] for j in range(8)], axis=1)
    gh, gl = split(gk)
    ub[cc, cz, cy] = dot_split(jnp.concatenate([gh, gl], axis=0), yh[pr], yl[pr], NT)
    u1 = [send(ub.at[cc, cz, cy], ub.at[cc, cz, cy], py[d]) for d in (1, 2, 3)]

    arrive(v_a2a)
    for j in range(8):
        f[:, 128 * j:128 * j + 128] = vr[j]

    def accumulate(p):
        nb = 5 if p < 4 else 4
        ch, cl = split(cag[p, :, :128 * nb] * scale)
        out = dot_split(ystk[:, 128 * p:128 * p + 128], ch, cl)
        for o in range(nb):
            j = (p + o) % 8
            f[:, 128 * j:128 * j + 128] += out[:, 128 * o:128 * o + 128]
        f[:, 128 * p:128 * p + 128] += dot_split(
            ystk[:, 128 * (p + 1):128 * (p + nb)], ch[:, 128:], cl[:, 128:], NT
        )

    def u_step(s):
        up, down = (cz - s) % 8, (cz + s) % 8
        if s < 3:
            u, w = ub.at[cc, up], ub.at[cc, down]
        else:
            u, w = ub.at[cc, up, pl.ds(0, 2)], ub.at[cc, down, pl.ds(2, 2)]
        return [send(u, u, z_up), send(w, w, z_down)]

    accumulate(4)
    arrive(u1)
    u2 = u_step(0)
    for s, p in ((1, 5), (2, 6), (3, 7)):
        arrive(g2[p])
        accumulate(p)
        arrive(u2)
        u2 = u_step(s)
    arrive(g2[0])
    accumulate(0)
    arrive(u2)
    u3 = send(ub.at[cc], ub.at[cc], sibling)
    for p in (1, 2, 3):
        arrive(g2[p])
        accumulate(p)

    def times_root(m):
        mh, ml = split(m)
        return dot_split(jnp.concatenate([mh, ml], axis=0), yh[...], yl[...])

    third = times_root(times_root(f[...]))
    yr = yb[cy, czh, cx]
    ro[0] = jnp.where(refresh[b_mine] == 1, 1.5 * yr - 0.5 * third, yr)

    panel = 2 * cy + czh
    rows_x = pl.ds(pl.multiple_of(cx * 32, 32), 32)

    def turned(block):
        tb[...] = block.T
        return tb[rows_x, :]

    for o in range(8):
        j = (panel + o) % 8
        if o < 4:
            c = cag[panel, rows_x, 128 * o:128 * o + 128]
        elif o == 4:
            q = panel % 4
            c = jnp.where(panel < 4, cag[q, rows_x, 512:640], turned(cag[q, :, 512:640]))
        else:
            c = turned(cag[j, :, 128 * (8 - o):128 * (8 - o) + 128])
        at = pl.ds(pl.multiple_of(j * 128, 128), 128)
        fo[0, :, at] = DECAY * rsh[:, at] + scale * c

    u3.wait_recv()
    for b in range(8):
        k = jnp.int32(0)
        for q in range(8):
            k = jnp.where(order[q] == b, q, k)
        for q in range(8):
            uo[0, :, 1024 * b + 128 * q:1024 * b + 128 * q + 128] = ub[k % 2, (q % 2) * 4 + k // 2, q // 2]

    for c in sent:
        c.wait_send()


def body(acts, rank_space_gradient, running_factor_blocks, inverse_root_blocks, owner_block_order, refresh):
    tokens_here = acts.shape[1]
    tokens = tokens_here * lax.axis_size("dp")
    hbm = pl.BlockSpec(memory_space=pl.ANY)
    smem = pl.BlockSpec(memory_space=pltpu.SMEM)
    vmem = pl.BlockSpec(memory_space=pltpu.VMEM)
    return pl.pallas_call(
        functools.partial(kernel, tokens),
        out_shape=(
            jax.ShapeDtypeStruct((1, 32, 1024), F32),
            jax.ShapeDtypeStruct((1, 32, 1024), F32),
            jax.ShapeDtypeStruct((1, 16, D), F32),
        ),
        in_specs=[smem, smem, hbm, hbm, hbm, hbm],
        out_specs=(vmem, vmem, vmem),
        scratch_shapes=[
            pltpu.VMEM((tokens_here, 1024), BF16),
            pltpu.VMEM((16, tokens_here), BF16),
            pltpu.VMEM((32, 1024), F32),
            pltpu.VMEM((4, 2, 4, 32, 1024), F32),
            pltpu.VMEM((1024, 1024), BF16),
            pltpu.VMEM((1024, 1024), BF16),
            pltpu.VMEM((64, 1536), BF16),
            pltpu.VMEM((8, 128, 640), F32),
            pltpu.VMEM((8, 3, 32, 640), F32),
            pltpu.VMEM((8, 32, 640), F32),
            pltpu.VMEM((8, 3, 8, 640), F32),
            pltpu.VMEM((8, 32, 640), F32),
            pltpu.VMEM((8, 32, 640), F32),
            pltpu.VMEM((2, 32, 640), F32),
            pltpu.VMEM((2, 32, 640), F32),
            pltpu.VMEM((8, 128, 640), F32),
            pltpu.VMEM((4, 8, 32, 128), F32),
            pltpu.VMEM((8, 32, 128), F32),
            pltpu.VMEM((8, 32, 128), F32),
            pltpu.VMEM((32, 1024), F32),
            pltpu.VMEM((128, 128), F32),
            pltpu.VMEM((2, 8, 4, 16, 128), F32),
            pltpu.SemaphoreType.DMA((8,)),
            pltpu.SemaphoreType.DMA((SEMS,)),
            pltpu.SemaphoreType.DMA((SEMS,)),
        ],
        compiler_params=pltpu.CompilerParams(
            collective_id=0, has_side_effects=True, vmem_limit_bytes=56 * 1024 * 1024
        ),
        cost_estimate=pl.CostEstimate(flops=8_000_000_000, bytes_accessed=12_000_000, transcendentals=0),
        name="kfac_step",
    )(
        owner_block_order,
        refresh,
        acts,
        jnp.swapaxes(rank_space_gradient[0], 0, 1),
        running_factor_blocks,
        inverse_root_blocks,
    )


def solution(mesh):
    return jax.shard_map(
        body,
        mesh=mesh,
        in_specs=(
            P(None, "dp", "mp"),
            P(None, "dp", None),
            P("mp", "dp", None),
            P("mp", "dp", None),
            P(),
            P(),
        ),
        out_specs=(P("mp", "dp", None), P("mp", "dp", None), P()),
        check_vma=False,
    )
```

```python
import functools

import jax
import jax.numpy as jnp
from jax import lax
from jax.experimental import pallas as pl
from jax.experimental.pallas import tpu as pltpu
from jax.sharding import PartitionSpec as P

D = 8192
DECAY = 0.75
DAMPING = 0.1
MESH = pl.DeviceIdType.MESH
NN = (((1,), (0,)), ((), ()))
NT = (((1,), (1,)), ((), ()))
TN = (((0,), (0,)), ((), ()))
SEMS = 200
F32 = jnp.float32
BF16 = jnp.bfloat16

GROUPS = ((4, 5, 6, 7), (0, 1, 2, 3))


def width(p):
    return 640 if p <= 4 else 512


def dot(a, b, dims=NN):
    return lax.dot_general(a, b, dims, preferred_element_type=F32)


def split(v):
    high = v.astype(BF16)
    return high, (v - high.astype(F32)).astype(BF16)


def dot_split(stacked, high, low, dims=NN):
    rows = stacked.shape[0] // 2
    both = dot(stacked, high, dims)
    return both[:rows] + both[rows:] + dot(stacked[:rows], low, dims)


def kernel(
    tokens,
    order, refresh, x_hbm, g_hbm, r_hbm, y_hbm,
    fo, ro, uo,
    x, g, rsh, yb, yh, yl, ystk, pan, r0, t1, r1, s1, r2, zb0, zb1, sibs, sibr, cag,
    rcol, vs, vr, f, tb, ub, lsem, ssem, rsem,
):
    scale = (1.0 - DECAY) / tokens
    zb = (zb0, zb1)
    dp = lax.axis_index("dp")
    mp = lax.axis_index("mp")
    cy, czh, cx = dp // 8, (dp // 4) % 2, dp % 4
    czl, cc = mp // 2, mp % 2
    cz = czh * 4 + czl

    def dev(y, zh, xx, zl, c):
        return {"dp": (y * 2 + zh) * 4 + xx, "mp": zl * 2 + c}

    def zdev(d):
        w = (cz + d) % 8
        return dev(cy, w // 4, cx, w % 4, cc)

    px = {d: dev(cy, czh, (cx + d) % 4, czl, cc) for d in (1, 2, 3)}
    py = {d: dev((cy + d) % 4, czh, cx, czl, cc) for d in (1, 2, 3)}
    pa = {
        (dz, dx): dev(cy, (czh + dz) % 2, (cx + dx) % 4, czl, cc)
        for dz in (0, 1) for dx in (0, 1, 2, 3) if dz or dx
    }
    pz = {d: zdev(d) for d in range(1, 8)}
    z_up, z_down = pz[1], pz[7]
    sibling = dev(cy, czh, cx, czl, 1 - cc)
    AX = {"x": (cx, px), "y": (cy, py)}

    count = [0]
    sent = []

    def send(src, dst, target):
        i = count[0]
        count[0] += 1
        copy = pltpu.make_async_remote_copy(
            src_ref=src, dst_ref=dst, send_sem=ssem.at[i], recv_sem=rsem.at[i],
            device_id=target, device_id_type=MESH,
        )
        copy.start()
        sent.append(copy)
        return copy

    def arrive(copies):
        for c in copies:
            c.wait_recv()

    own_y = yb.at[cy, czh, cx]
    load_y = pltpu.make_async_copy(y_hbm.at[0], own_y, lsem.at[0])
    load_r = pltpu.make_async_copy(r_hbm.at[0], rsh, lsem.at[1])
    load_y.start()
    load_r.start()
    nk = 4
    depth = x.shape[0] // nk
    load_x = [
        pltpu.make_async_copy(x_hbm.at[0, pl.ds(i * depth, depth)], x.at[pl.ds(i * depth, depth)], lsem.at[3 + i])
        for i in range(nk)
    ]
    for c in load_x:
        c.start()
    load_g = pltpu.make_async_copy(g_hbm, g, lsem.at[2])
    load_g.start()

    barrier = pltpu.get_barrier_semaphore()
    peers = list(pa.values()) + list(py.values()) + [pz[d] for d in (1, 2, 3, 5, 6, 7)] + [sibling]
    for peer in peers:
        pl.semaphore_signal(barrier, inc=1, device_id=peer, device_id_type=MESH)
    pl.semaphore_wait(barrier, len(peers))

    def y_first(h):
        a = [send(yb.at[cy, h, cx, pl.ds(0, 16)], yb.at[cy, h, cx, pl.ds(0, 16)], px[d]) for d in (1, 2, 3)]
        b = [send(yb.at[cy, h, cx, pl.ds(16, 16)], yb.at[cy, h, cx, pl.ds(16, 16)], py[d]) for d in (1, 2, 3)]
        return a + b

    def y_second(h):
        a = [send(yb.at[cy, h, :, pl.ds(0, 16)], yb.at[cy, h, :, pl.ds(0, 16)], py[d]) for d in (1, 3)]
        b = [send(yb.at[:, h, cx, pl.ds(16, 16)], yb.at[:, h, cx, pl.ds(16, 16)], px[d]) for d in (1, 3)]
        return a + b

    def y_third(h, copies):
        arrive(copies)
        out = []
        for d, at in ((3, 0), (1, 8)):
            ya, xa = (cy + d) % 4, (cx + d) % 4
            ref = yb.at[ya, h, :, pl.ds(at, 8)]
            out.append(send(ref, ref, py[4 - d]))
            ref = yb.at[:, h, xa, pl.ds(16 + at, 8)]
            out.append(send(ref, ref, px[4 - d]))
        return out

    my_j = czh * 4 + cx
    load_y.wait()
    y_z = send(own_y, own_y, pa[(1, 0)])
    y_own1 = y_first(czh)
    load_r.wait()
    r_a2a = []
    for (dz, dx), peer in pa.items():
        j = ((czh + dz) % 2) * 4 + (cx + dx) % 4
        r_a2a.append(
            send(rsh.at[:, pl.ds(pl.multiple_of(j * 128, 128), 128)], rcol.at[cy, my_j], peer)
        )
    rcol[cy, my_j] = rsh[:, pl.ds(pl.multiple_of(my_j * 128, 128), 128)]

    yr = yb[cy, czh, cx]
    yrh, yrl = split(yr)
    ystk[0:32, 0:1024] = yrh
    ystk[0:32, 1024:1536] = yrh[:, :512]
    ystk[32:64, 0:1024] = yrl
    ystk[32:64, 1024:1536] = yrl[:, :512]

    def gemm(i, k0, kn, first):
        lo = 256 * i
        n = 768 if i < 2 else 640
        segs = [(lo, n, 0)] if lo + n <= 1024 else [(lo, 1024 - lo, 0), (0, lo + n - 1024, 1024 - lo)]
        for start, w, at in segs:
            v = dot(x[k0:k0 + kn, lo:lo + 256], x[k0:k0 + kn, start:start + w], TN)
            for half in (0, 1):
                p = 2 * i + half
                cols = 640 if p < 4 else 512
                b0, b1 = max(at, 128 * half), min(at + w, 128 * half + cols)
                if b1 <= b0:
                    continue
                part = v[128 * half:128 * half + 128, b0 - at:b1 - at]
                c0 = b0 - 128 * half
                if first:
                    pan[p, :, c0:c0 + b1 - b0] = part
                else:
                    pan[p, :, c0:c0 + b1 - b0] += part

    ax1 = {p: AX["x" if p % 2 == 0 else "y"] for p in range(8)}
    ax2 = {p: AX["y" if p % 2 == 0 else "x"] for p in range(8)}

    def quarter(a, at=0, rows=32):
        return pl.ds(pl.multiple_of((a % 4) * 32 + at, 8), rows)

    def rs_first(p):
        a, peer = ax1[p]
        w = pl.ds(0, width(p))
        return [
            send(pan.at[p, quarter(a + 2, 16 * i, 16), w], r0.at[p, i, :, w], peer[d]) for i, d in ((0, 1), (1, 3))
        ]

    def rs_mid(p, copies):
        arrive(copies)
        a, peer = ax1[p]
        w = width(p)
        out = []
        for i, d in ((0, 1), (1, 3)):
            t1[p, i, 16 * i:16 * i + 16, :w] = pan[p, quarter(a + d, 16 * i, 16), :w] + r0[p, i, :, :w]
            t1[p, i, 16 - 16 * i:32 - 16 * i, :w] = pan[p, quarter(a + d, 16 - 16 * i, 16), :w]
            out.append(send(t1.at[p, i, :, pl.ds(0, w)], r1.at[p, i, :, pl.ds(0, w)], peer[d]))
        return out

    def rs_second(p, copies):
        arrive(copies)
        a, _ = ax1[p]
        b, peer = ax2[p]
        w = width(p)
        s1[p, :, :w] = pan[p, quarter(a), :w] + r1[p, 0, :, :w] + r1[p, 1, :, :w]
        return [
            send(
                s1.at[p, pl.ds(pl.multiple_of(((b + d) % 4) * 8, 8), 8), pl.ds(0, w)],
                r2.at[p, d - 1, :, pl.ds(0, w)], peer[d],
            )
            for d in (1, 2, 3)
        ]

    def rs_end(p, copies):
        arrive(copies)
        b, _ = ax2[p]
        w = width(p)
        gi = 0 if p >= 4 else 1
        i = p % 4
        zb[gi][cz, 8 * i:8 * i + 8, :w] = (
            s1[p, pl.ds(pl.multiple_of(b * 8, 8), 8), :w] + r2[p, 0, :, :w] + r2[p, 1, :, :w] + r2[p, 2, :, :w]
        )
        if w < 640:
            zb[gi][cz, 8 * i:8 * i + 8, w:640] = jnp.zeros((8, 640 - w), F32)

    def z_step(gi, s):
        up, down = (cz - s) % 8, (cz + s) % 8
        if s < 3:
            u, v = zb[gi].at[up], zb[gi].at[down]
        else:
            u, v = zb[gi].at[up, pl.ds(0, 16)], zb[gi].at[down, pl.ds(16, 16)]
        return [send(u, u, z_up), send(v, v, z_down)]

    b_mine = order[2 * czl + cc]
    b_other = order[2 * czl + 1 - cc]

    def picked(gi, b):
        return zb[gi][b // 2] + zb[gi][b // 2 + 4]

    def to_sibling(gi):
        sibs[gi] = jnp.where(b_other % 2 == cc, picked(gi, b_other), 0.0)
        return [send(sibs.at[gi], sibr.at[gi], sibling)]

    def take(gi):
        v = jnp.where(b_mine % 2 == cc, picked(gi, b_mine), sibr[gi])
        for i, p in enumerate(GROUPS[gi]):
            a, _ = ax1[p]
            b, _ = ax2[p]
            w = width(p)
            cag[p, pl.ds(pl.multiple_of(a * 32 + b * 8, 8), 8), :w] = v[8 * i:8 * i + 8, :w]

    def ag_first(p):
        a, _ = ax1[p]
        b, peer = ax2[p]
        ref = cag.at[p, pl.ds(pl.multiple_of(a * 32 + b * 8, 8), 8), pl.ds(0, width(p))]
        return [send(ref, ref, peer[d]) for d in (1, 2, 3)]

    def ag_second(p, copies):
        arrive(copies)
        a, peer = ax1[p]
        ref = cag.at[p, quarter(a), pl.ds(0, width(p))]
        return [send(ref, ref, peer[d]) for d in (1, 3)]

    def ag_third(p, copies):
        arrive(copies)
        a, peer = ax1[p]
        out = []
        for d, at in ((3, 0), (1, 16)):
            ref = cag.at[p, quarter(a + d, at, 16), pl.ds(0, width(p))]
            out.append(send(ref, ref, peer[4 - d]))
        return out

    c1, cm, c2, g1, g2, g3 = {}, {}, {}, {}, {}, {}
    ga, gb = GROUPS
    for k in range(nk):
        load_x[k].wait()
        gemm(2, k * depth, depth, k == 0)
    load_g.wait()
    grads = dot(g[...], x[...])
    for j in range(8):
        pan[4, 16 * j:16 * j + 16, 512:640] = grads[:, 128 * j:128 * j + 128]
    for p in (4, 5):
        c1[p] = rs_first(p)
    y_z.wait_recv()
    y_oth1 = y_first(1 - czh)
    gemm(3, 0, x.shape[0], True)
    for p in (6, 7):
        c1[p] = rs_first(p)
    for p in (4, 5):
        cm[p] = rs_mid(p, c1[p])
    gemm(0, 0, x.shape[0], True)
    for p in (0, 1):
        c1[p] = rs_first(p)
    for p in (6, 7):
        cm[p] = rs_mid(p, c1[p])
    for p in (4, 5):
        c2[p] = rs_second(p, cm[p])
    gemm(1, 0, x.shape[0], True)
    for p in (2, 3):
        c1[p] = rs_first(p)
    for p in (0, 1):
        cm[p] = rs_mid(p, c1[p])
    for p in (6, 7):
        c2[p] = rs_second(p, cm[p])
    for p in ga:
        rs_end(p, c2[p])
    za = z_step(0, 0)
    for p in (2, 3):
        cm[p] = rs_mid(p, c1[p])
    arrive(y_own1)
    y_own2 = y_second(czh)
    arrive(za)
    za = z_step(0, 1)
    for p in (0, 1):
        c2[p] = rs_second(p, cm[p])
    arrive(za)
    za = z_step(0, 2)
    for p in (2, 3):
        c2[p] = rs_second(p, cm[p])
    for p in gb:
        rs_end(p, c2[p])
    zc = z_step(1, 0)
    arrive(za)
    za = z_step(0, 3)
    y_own3 = y_third(czh, y_own2)
    arrive(y_oth1)
    y_oth2 = y_second(1 - czh)
    arrive(zc)
    zc = z_step(1, 1)
    arrive(za)
    sa = to_sibling(0)
    arrive(zc)
    zc = z_step(1, 2)
    arrive(sa)
    take(0)
    for p in ga:
        g1[p] = ag_first(p)
    arrive(r_a2a)
    r_y = [send(rcol.at[cy], rcol.at[cy], py[d]) for d in (1, 2, 3)]
    arrive(zc)
    zc = z_step(1, 3)
    for p in ga:
        g2[p] = ag_second(p, g1[p])
    arrive(zc)
    sb = to_sibling(1)
    for p in ga:
        g3[p] = ag_third(p, g2[p])
    arrive(sb)
    take(1)
    for p in gb:
        g1[p] = ag_first(p)
    y_oth3 = y_third(1 - czh, y_oth2)
    for p in gb:
        g2[p] = ag_second(p, g1[p])

    arrive(y_own3)
    arrive(g3[4])
    gk = jnp.concatenate([cag[4, 16 * j:16 * j + 16, 512:640] for j in range(8)], axis=1)
    gh, gl = split(gk)
    ph, plow = split(yb[cy, czh].reshape(128, 1024))
    ub[cc, cz, cy] = dot_split(jnp.concatenate([gh, gl], axis=0), ph, plow, NT)
    u1 = [send(ub.at[cc, cz, cy], ub.at[cc, cz, cy], py[d]) for d in (1, 2, 3)]

    def accumulate(p):
        nb = 5 if p < 4 else 4
        ch, cl = split(cag[p, :, :128 * nb] * scale)
        out = dot_split(ystk[:, 128 * p:128 * p + 128], ch, cl)
        for o in range(nb):
            j = (p + o) % 8
            f[:, 128 * j:128 * j + 128] += out[:, 128 * o:128 * o + 128]
        f[:, 128 * p:128 * p + 128] += dot_split(
            ystk[:, 128 * (p + 1):128 * (p + nb)], ch[:, 128:], cl[:, 128:], NT
        )

    f[...] = jnp.zeros_like(f)
    accumulate(4)
    for p in (5, 6, 7):
        arrive(g3[p])
        accumulate(p)
    arrive(u1)
    u2 = [send(ub.at[cc, cz], ub.at[cc, cz], pz[d]) for d in range(1, 8)]
    for p in gb:
        g3[p] = ag_third(p, g2[p])

    arrive(y_oth3)

    def convert(i, carry):
        v = yb[i // 8, (i // 4) % 2, i % 4]
        h, l = split(v)
        at = pl.ds(pl.multiple_of(i * 32, 32), 32)
        yh[at] = h
        yl[at] = l
        return carry

    lax.fori_loop(0, 32, convert, 0)
    arrive(r_y)
    n = 1024
    eye = (
        lax.broadcasted_iota(jnp.int32, (n, 128), 0) == lax.broadcasted_iota(jnp.int32, (n, 128), 1) + my_j * 128
    )
    rh, rl = split(DECAY * rcol[...].reshape(n, 128) + jnp.where(eye, DAMPING, 0.0))
    rows_i = pl.ds(pl.multiple_of(cy * 256, 256), 256)
    v = dot(yh[rows_i], rh) + dot(yl[rows_i], rh) + dot(yh[rows_i], rl)
    vs[...] = v.reshape(8, 32, 128)
    v_a2a = []
    for (dz, dx), peer in pa.items():
        j = ((czh + dz) % 2) * 4 + (cx + dx) % 4
        v_a2a.append(send(vs.at[j], vr.at[my_j], peer))
    vr[my_j] = vs[my_j]

    arrive(u2)
    u3 = send(ub.at[cc], ub.at[cc], sibling)
    for p in gb:
        arrive(g3[p])
        accumulate(p)
    arrive(v_a2a)
    for j in range(8):
        f[:, 128 * j:128 * j + 128] += vr[j]

    def times_root(m):
        mh, ml = split(m)
        return dot_split(jnp.concatenate([mh, ml], axis=0), yh[...], yl[...])

    third = times_root(times_root(f[...]))
    yr = yb[cy, czh, cx]
    ro[0] = jnp.where(refresh[b_mine] == 1, 1.5 * yr - 0.5 * third, yr)

    panel = 2 * cy + czh
    rows_x = pl.ds(pl.multiple_of(cx * 32, 32), 32)

    def turned(block):
        tb[...] = block.T
        return tb[rows_x, :]

    for o in range(8):
        j = (panel + o) % 8
        if o < 4:
            c = cag[panel, rows_x, 128 * o:128 * o + 128]
        elif o == 4:
            q = panel % 4
            c = jnp.where(panel < 4, cag[q, rows_x, 512:640], turned(cag[q, :, 512:640]))
        else:
            c = turned(cag[j, :, 128 * (8 - o):128 * (8 - o) + 128])
        at = pl.ds(pl.multiple_of(j * 128, 128), 128)
        fo[0, :, at] = DECAY * rsh[:, at] + scale * c

    u3.wait_recv()
    for b in range(8):
        k = jnp.int32(0)
        for q in range(8):
            k = jnp.where(order[q] == b, q, k)
        for q in range(8):
            uo[0, :, 1024 * b + 128 * q:1024 * b + 128 * q + 128] = ub[k % 2, (q % 2) * 4 + k // 2, q // 2]

    for c in sent:
        c.wait_send()


def body(acts, rank_space_gradient, running_factor_blocks, inverse_root_blocks, owner_block_order, refresh):
    tokens_here = acts.shape[1]
    tokens = tokens_here * lax.axis_size("dp")
    hbm = pl.BlockSpec(memory_space=pl.ANY)
    smem = pl.BlockSpec(memory_space=pltpu.SMEM)
    vmem = pl.BlockSpec(memory_space=pltpu.VMEM)
    return pl.pallas_call(
        functools.partial(kernel, tokens),
        out_shape=(
            jax.ShapeDtypeStruct((1, 32, 1024), F32),
            jax.ShapeDtypeStruct((1, 32, 1024), F32),
            jax.ShapeDtypeStruct((1, 16, D), F32),
        ),
        in_specs=[smem, smem, hbm, hbm, hbm, hbm],
        out_specs=(vmem, vmem, vmem),
        scratch_shapes=[
            pltpu.VMEM((tokens_here, 1024), BF16),
            pltpu.VMEM((16, tokens_here), BF16),
            pltpu.VMEM((32, 1024), F32),
            pltpu.VMEM((4, 2, 4, 32, 1024), F32),
            pltpu.VMEM((1024, 1024), BF16),
            pltpu.VMEM((1024, 1024), BF16),
            pltpu.VMEM((64, 1536), BF16),
            pltpu.VMEM((8, 128, 640), F32),
            pltpu.VMEM((8, 2, 16, 640), F32),
            pltpu.VMEM((8, 2, 32, 640), F32),
            pltpu.VMEM((8, 2, 32, 640), F32),
            pltpu.VMEM((8, 32, 640), F32),
            pltpu.VMEM((8, 3, 8, 640), F32),
            pltpu.VMEM((8, 32, 640), F32),
            pltpu.VMEM((8, 32, 640), F32),
            pltpu.VMEM((2, 32, 640), F32),
            pltpu.VMEM((2, 32, 640), F32),
            pltpu.VMEM((8, 128, 640), F32),
            pltpu.VMEM((4, 8, 32, 128), F32),
            pltpu.VMEM((8, 32, 128), F32),
            pltpu.VMEM((8, 32, 128), F32),
            pltpu.VMEM((32, 1024), F32),
            pltpu.VMEM((128, 128), F32),
            pltpu.VMEM((2, 8, 4, 16, 128), F32),
            pltpu.SemaphoreType.DMA((8,)),
            pltpu.SemaphoreType.DMA((SEMS,)),
            pltpu.SemaphoreType.DMA((SEMS,)),
        ],
        compiler_params=pltpu.CompilerParams(
            collective_id=0, has_side_effects=True, vmem_limit_bytes=56 * 1024 * 1024
        ),
        cost_estimate=pl.CostEstimate(flops=8_000_000_000, bytes_accessed=12_000_000, transcendentals=0),
        name="kfac_step",
    )(
        owner_block_order,
        refresh,
        acts,
        jnp.swapaxes(rank_space_gradient[0], 0, 1),
        running_factor_blocks,
        inverse_root_blocks,
    )


def solution(mesh):
    return jax.shard_map(
        body,
        mesh=mesh,
        in_specs=(
            P(None, "dp", "mp"),
            P(None, "dp", None),
            P("mp", "dp", None),
            P("mp", "dp", None),
            P(),
            P(),
        ),
        out_specs=(P("mp", "dp", None), P("mp", "dp", None), P()),
        check_vma=False,
    )
```

```python
import functools

import jax
import jax.numpy as jnp
from jax import lax
from jax.experimental import pallas as pl
from jax.experimental.pallas import tpu as pltpu
from jax.sharding import PartitionSpec as P

D = 8192
DECAY = 0.75
DAMPING = 0.1
MESH = pl.DeviceIdType.MESH
NN = (((1,), (0,)), ((), ()))
NT = (((1,), (1,)), ((), ()))
TN = (((0,), (0,)), ((), ()))
SEMS = 200
F32 = jnp.float32
BF16 = jnp.bfloat16

GROUPS = ((4, 5, 6, 7), (0, 1, 2, 3))


def width(p):
    return 640 if p <= 4 else 512


def dot(a, b, dims=NN):
    return lax.dot_general(a, b, dims, preferred_element_type=F32)


def split(v):
    high = v.astype(BF16)
    return high, (v - high.astype(F32)).astype(BF16)


def dot_split(stacked, high, low, dims=NN):
    rows = stacked.shape[0] // 2
    both = dot(stacked, high, dims)
    return both[:rows] + both[rows:] + dot(stacked[:rows], low, dims)


def kernel(
    tokens,
    order, refresh, x_hbm, g_hbm, r_hbm, y_hbm,
    both, uo,
    x, g, rsh, yb, yh, yl, ystk, pan, r0, t1, r1, s1, r2, zb0, zb1, sibs, sibr, cag,
    rcol, vs, vr, f, tb, ub, lsem, ssem, rsem,
):
    scale = (1.0 - DECAY) / tokens
    zb = (zb0, zb1)
    dp = lax.axis_index("dp")
    mp = lax.axis_index("mp")
    cy, czh, cx = dp // 8, (dp // 4) % 2, dp % 4
    czl, cc = mp // 2, mp % 2
    cz = czh * 4 + czl

    def dev(y, zh, xx, zl, c):
        return {"dp": (y * 2 + zh) * 4 + xx, "mp": zl * 2 + c}

    def zdev(d):
        w = (cz + d) % 8
        return dev(cy, w // 4, cx, w % 4, cc)

    px = {d: dev(cy, czh, (cx + d) % 4, czl, cc) for d in (1, 2, 3)}
    py = {d: dev((cy + d) % 4, czh, cx, czl, cc) for d in (1, 2, 3)}
    pa = {
        (dz, dx): dev(cy, (czh + dz) % 2, (cx + dx) % 4, czl, cc)
        for dz in (0, 1) for dx in (0, 1, 2, 3) if dz or dx
    }
    pz = {d: zdev(d) for d in range(1, 8)}
    z_up, z_down = pz[1], pz[7]
    sibling = dev(cy, czh, cx, czl, 1 - cc)
    AX = {"x": (cx, px), "y": (cy, py)}

    count = [0]
    sent = []

    def send(src, dst, target):
        i = count[0]
        count[0] += 1
        copy = pltpu.make_async_remote_copy(
            src_ref=src, dst_ref=dst, send_sem=ssem.at[i], recv_sem=rsem.at[i],
            device_id=target, device_id_type=MESH,
        )
        copy.start()
        sent.append(copy)
        return copy

    def arrive(copies):
        for c in copies:
            c.wait_recv()

    own_y = yb.at[cy, czh, cx]
    load_y = pltpu.make_async_copy(y_hbm.at[0], own_y, lsem.at[0])
    load_r = pltpu.make_async_copy(r_hbm.at[0], rsh, lsem.at[1])
    load_y.start()
    load_r.start()
    nk = 4
    depth = x.shape[0] // nk
    load_x = [
        pltpu.make_async_copy(x_hbm.at[0, pl.ds(i * depth, depth)], x.at[pl.ds(i * depth, depth)], lsem.at[3 + i])
        for i in range(nk)
    ]
    for c in load_x:
        c.start()
    load_g = pltpu.make_async_copy(g_hbm, g, lsem.at[2])
    load_g.start()

    barrier = pltpu.get_barrier_semaphore()
    peers = list(pa.values()) + list(py.values()) + [pz[d] for d in (1, 2, 3, 5, 6, 7)] + [sibling]
    for peer in peers:
        pl.semaphore_signal(barrier, inc=1, device_id=peer, device_id_type=MESH)
    pl.semaphore_wait(barrier, len(peers))

    def y_first(h):
        a = [send(yb.at[cy, h, cx, pl.ds(0, 16)], yb.at[cy, h, cx, pl.ds(0, 16)], px[d]) for d in (1, 2, 3)]
        b = [send(yb.at[cy, h, cx, pl.ds(16, 16)], yb.at[cy, h, cx, pl.ds(16, 16)], py[d]) for d in (1, 2, 3)]
        return a + b

    def y_second(h):
        a = [send(yb.at[cy, h, :, pl.ds(0, 16)], yb.at[cy, h, :, pl.ds(0, 16)], py[d]) for d in (1, 3)]
        b = [send(yb.at[:, h, cx, pl.ds(16, 16)], yb.at[:, h, cx, pl.ds(16, 16)], px[d]) for d in (1, 3)]
        return a + b

    def y_third(h, copies):
        arrive(copies)
        out = []
        for d, at in ((3, 0), (1, 8)):
            ya, xa = (cy + d) % 4, (cx + d) % 4
            ref = yb.at[ya, h, :, pl.ds(at, 8)]
            out.append(send(ref, ref, py[4 - d]))
            ref = yb.at[:, h, xa, pl.ds(16 + at, 8)]
            out.append(send(ref, ref, px[4 - d]))
        return out

    my_j = czh * 4 + cx
    load_y.wait()
    y_z = send(own_y, own_y, pa[(1, 0)])
    y_own1 = y_first(czh)
    load_r.wait()
    r_a2a = []
    for (dz, dx), peer in pa.items():
        j = ((czh + dz) % 2) * 4 + (cx + dx) % 4
        r_a2a.append(
            send(rsh.at[:, pl.ds(pl.multiple_of(j * 128, 128), 128)], rcol.at[cy, my_j], peer)
        )
    rcol[cy, my_j] = rsh[:, pl.ds(pl.multiple_of(my_j * 128, 128), 128)]

    yr = yb[cy, czh, cx]
    yrh, yrl = split(yr)
    ystk[0:32, 0:1024] = yrh
    ystk[0:32, 1024:1536] = yrh[:, :512]
    ystk[32:64, 0:1024] = yrl
    ystk[32:64, 1024:1536] = yrl[:, :512]

    def gemm(i, k0, kn, first):
        lo = 256 * i
        n = 768 if i < 2 else 640
        segs = [(lo, n, 0)] if lo + n <= 1024 else [(lo, 1024 - lo, 0), (0, lo + n - 1024, 1024 - lo)]
        for start, w, at in segs:
            v = dot(x[k0:k0 + kn, lo:lo + 256], x[k0:k0 + kn, start:start + w], TN)
            for half in (0, 1):
                p = 2 * i + half
                cols = 640 if p < 4 else 512
                b0, b1 = max(at, 128 * half), min(at + w, 128 * half + cols)
                if b1 <= b0:
                    continue
                part = v[128 * half:128 * half + 128, b0 - at:b1 - at]
                c0 = b0 - 128 * half
                if first:
                    pan[p, :, c0:c0 + b1 - b0] = part
                else:
                    pan[p, :, c0:c0 + b1 - b0] += part

    ax1 = {p: AX["x" if p % 2 == 0 else "y"] for p in range(8)}
    ax2 = {p: AX["y" if p % 2 == 0 else "x"] for p in range(8)}

    def quarter(a, at=0, rows=32):
        return pl.ds(pl.multiple_of((a % 4) * 32 + at, 8), rows)

    def rs_first(p):
        a, peer = ax1[p]
        w = pl.ds(0, width(p))
        return [
            send(pan.at[p, quarter(a + 2, 16 * i, 16), w], r0.at[p, i, :, w], peer[d]) for i, d in ((0, 1), (1, 3))
        ]

    def rs_mid(p, copies):
        arrive(copies)
        a, peer = ax1[p]
        w = width(p)
        out = []
        for i, d in ((0, 1), (1, 3)):
            t1[p, i, 16 * i:16 * i + 16, :w] = pan[p, quarter(a + d, 16 * i, 16), :w] + r0[p, i, :, :w]
            t1[p, i, 16 - 16 * i:32 - 16 * i, :w] = pan[p, quarter(a + d, 16 - 16 * i, 16), :w]
            out.append(send(t1.at[p, i, :, pl.ds(0, w)], r1.at[p, i, :, pl.ds(0, w)], peer[d]))
        return out

    def rs_second(p, copies):
        arrive(copies)
        a, _ = ax1[p]
        b, peer = ax2[p]
        w = width(p)
        s1[p, :, :w] = pan[p, quarter(a), :w] + r1[p, 0, :, :w] + r1[p, 1, :, :w]
        return [
            send(
                s1.at[p, pl.ds(pl.multiple_of(((b + d) % 4) * 8, 8), 8), pl.ds(0, w)],
                r2.at[p, d - 1, :, pl.ds(0, w)], peer[d],
            )
            for d in (1, 2, 3)
        ]

    def rs_end(p, copies):
        arrive(copies)
        b, _ = ax2[p]
        w = width(p)
        gi = 0 if p >= 4 else 1
        i = p % 4
        zb[gi][cz, 8 * i:8 * i + 8, :w] = (
            s1[p, pl.ds(pl.multiple_of(b * 8, 8), 8), :w] + r2[p, 0, :, :w] + r2[p, 1, :, :w] + r2[p, 2, :, :w]
        )
        if w < 640:
            zb[gi][cz, 8 * i:8 * i + 8, w:640] = jnp.zeros((8, 640 - w), F32)

    def z_step(gi, s):
        up, down = (cz - s) % 8, (cz + s) % 8
        if s < 3:
            u, v = zb[gi].at[up], zb[gi].at[down]
        else:
            u, v = zb[gi].at[up, pl.ds(0, 16)], zb[gi].at[down, pl.ds(16, 16)]
        return [send(u, u, z_up), send(v, v, z_down)]

    b_mine = order[2 * czl + cc]
    b_other = order[2 * czl + 1 - cc]

    def picked(gi, b):
        return zb[gi][b // 2] + zb[gi][b // 2 + 4]

    def to_sibling(gi):
        sibs[gi] = jnp.where(b_other % 2 == cc, picked(gi, b_other), 0.0)
        return [send(sibs.at[gi], sibr.at[gi], sibling)]

    def take(gi):
        v = jnp.where(b_mine % 2 == cc, picked(gi, b_mine), sibr[gi])
        for i, p in enumerate(GROUPS[gi]):
            a, _ = ax1[p]
            b, _ = ax2[p]
            w = width(p)
            cag[p, pl.ds(pl.multiple_of(a * 32 + b * 8, 8), 8), :w] = v[8 * i:8 * i + 8, :w]

    def ag_first(p):
        a, _ = ax1[p]
        b, peer = ax2[p]
        ref = cag.at[p, pl.ds(pl.multiple_of(a * 32 + b * 8, 8), 8), pl.ds(0, width(p))]
        return [send(ref, ref, peer[d]) for d in (1, 2, 3)]

    def ag_second(p, copies):
        arrive(copies)
        a, peer = ax1[p]
        ref = cag.at[p, quarter(a), pl.ds(0, width(p))]
        return [send(ref, ref, peer[d]) for d in (1, 3)]

    def ag_third(p, copies):
        arrive(copies)
        a, peer = ax1[p]
        out = []
        for d, at in ((3, 0), (1, 16)):
            ref = cag.at[p, quarter(a + d, at, 16), pl.ds(0, width(p))]
            out.append(send(ref, ref, peer[4 - d]))
        return out

    c1, cm, c2, g1, g2, g3 = {}, {}, {}, {}, {}, {}
    ga, gb = GROUPS
    for k in range(nk):
        load_x[k].wait()
        gemm(2, k * depth, depth, k == 0)
    load_g.wait()
    grads = dot(g[...], x[...])
    for j in range(8):
        pan[4, 16 * j:16 * j + 16, 512:640] = grads[:, 128 * j:128 * j + 128]
    for p in (4, 5):
        c1[p] = rs_first(p)
    y_z.wait_recv()
    y_oth1 = y_first(1 - czh)
    gemm(3, 0, x.shape[0], True)
    for p in (6, 7):
        c1[p] = rs_first(p)
    for p in (4, 5):
        cm[p] = rs_mid(p, c1[p])
    gemm(0, 0, x.shape[0], True)
    for p in (0, 1):
        c1[p] = rs_first(p)
    for p in (6, 7):
        cm[p] = rs_mid(p, c1[p])
    for p in (4, 5):
        c2[p] = rs_second(p, cm[p])
    gemm(1, 0, x.shape[0], True)
    for p in (2, 3):
        c1[p] = rs_first(p)
    for p in (0, 1):
        cm[p] = rs_mid(p, c1[p])
    for p in (6, 7):
        c2[p] = rs_second(p, cm[p])
    for p in ga:
        rs_end(p, c2[p])
    za = z_step(0, 0)
    for p in (2, 3):
        cm[p] = rs_mid(p, c1[p])
    arrive(r_a2a)
    r_y = [send(rcol.at[cy], rcol.at[cy], py[d]) for d in (1, 2, 3)]
    arrive(y_own1)
    y_own2 = y_second(czh)
    arrive(za)
    za = z_step(0, 1)
    for p in (0, 1):
        c2[p] = rs_second(p, cm[p])
    arrive(za)
    za = z_step(0, 2)
    for p in (2, 3):
        c2[p] = rs_second(p, cm[p])
    for p in gb:
        rs_end(p, c2[p])
    zc = z_step(1, 0)
    arrive(za)
    za = z_step(0, 3)
    y_own3 = y_third(czh, y_own2)
    arrive(y_oth1)
    y_oth2 = y_second(1 - czh)
    arrive(zc)
    zc = z_step(1, 1)
    arrive(za)
    sa = to_sibling(0)
    arrive(zc)
    zc = z_step(1, 2)
    arrive(sa)
    take(0)
    for p in ga:
        g1[p] = ag_first(p)
    arrive(zc)
    zc = z_step(1, 3)
    for p in ga:
        g2[p] = ag_second(p, g1[p])
    arrive(zc)
    sb = to_sibling(1)
    for p in ga:
        g3[p] = ag_third(p, g2[p])
    arrive(sb)
    take(1)
    for p in gb:
        g1[p] = ag_first(p)
    y_oth3 = y_third(1 - czh, y_oth2)
    for p in gb:
        g2[p] = ag_second(p, g1[p])

    arrive(y_own3)
    arrive(g3[4])
    gk = jnp.concatenate([cag[4, 16 * j:16 * j + 16, 512:640] for j in range(8)], axis=1)
    gh, gl = split(gk)
    ph, plow = split(yb[cy, czh].reshape(128, 1024))
    cond = dot_split(jnp.concatenate([gh, gl], axis=0), ph, plow, NT)
    ub[cc, cz, cy] = cond
    u1 = [send(ub.at[cc, cz, cy], ub.at[cc, cz, cy], pz[d]) for d in range(1, 8)]

    def accumulate(p):
        nb = 5 if p < 4 else 4
        ch, cl = split(cag[p, :, :128 * nb] * scale)
        out = dot_split(ystk[:, 128 * p:128 * p + 128], ch, cl)
        for o in range(nb):
            j = (p + o) % 8
            f[:, 128 * j:128 * j + 128] += out[:, 128 * o:128 * o + 128]
        f[:, 128 * p:128 * p + 128] += dot_split(
            ystk[:, 128 * (p + 1):128 * (p + nb)], ch[:, 128:], cl[:, 128:], NT
        )

    f[...] = jnp.zeros_like(f)
    accumulate(4)
    for p in (5, 6, 7):
        arrive(g3[p])
        accumulate(p)
    arrive(u1)
    u2 = [send(ub.at[cc, :, cy], ub.at[cc, :, cy], py[d]) for d in (1, 2, 3)]
    for p in gb:
        g3[p] = ag_third(p, g2[p])

    arrive(y_oth3)

    def convert(i, carry):
        v = yb[i // 8, (i // 4) % 2, i % 4]
        h, l = split(v)
        at = pl.ds(pl.multiple_of(i * 32, 32), 32)
        yh[at] = h
        yl[at] = l
        return carry

    lax.fori_loop(0, 32, convert, 0)
    arrive(r_y)
    n = 1024
    eye = (
        lax.broadcasted_iota(jnp.int32, (n, 128), 0) == lax.broadcasted_iota(jnp.int32, (n, 128), 1) + my_j * 128
    )
    rh, rl = split(DECAY * rcol[...].reshape(n, 128) + jnp.where(eye, DAMPING, 0.0))
    rows_i = pl.ds(pl.multiple_of(cy * 256, 256), 256)
    v = dot(yh[rows_i], rh) + dot(yl[rows_i], rh) + dot(yh[rows_i], rl)
    vs[...] = v.reshape(8, 32, 128)
    v_a2a = []
    for (dz, dx), peer in pa.items():
        j = ((czh + dz) % 2) * 4 + (cx + dx) % 4
        v_a2a.append(send(vs.at[j], vr.at[my_j], peer))
    vr[my_j] = vs[my_j]

    arrive(u2)
    u3 = send(ub.at[cc], ub.at[cc], sibling)
    for p in gb:
        arrive(g3[p])
        accumulate(p)
    arrive(v_a2a)
    for j in range(8):
        f[:, 128 * j:128 * j + 128] += vr[j]

    def times_root(m):
        mh, ml = split(m)
        return dot_split(jnp.concatenate([mh, ml], axis=0), yh[...], yl[...])

    third = times_root(times_root(f[...]))
    yr = yb[cy, czh, cx]
    both[1] = jnp.where(refresh[b_mine] == 1, 1.5 * yr - 0.5 * third, yr)

    panel = 2 * cy + czh
    rows_x = pl.ds(pl.multiple_of(cx * 32, 32), 32)

    def turned(block):
        tb[...] = block.T
        return tb[rows_x, :]

    for o in range(8):
        j = (panel + o) % 8
        if o < 4:
            c = cag[panel, rows_x, 128 * o:128 * o + 128]
        elif o == 4:
            q = panel % 4
            c = jnp.where(panel < 4, cag[q, rows_x, 512:640], turned(cag[q, :, 512:640]))
        else:
            c = turned(cag[j, :, 128 * (8 - o):128 * (8 - o) + 128])
        at = pl.ds(pl.multiple_of(j * 128, 128), 128)
        both[0, :, at] = DECAY * rsh[:, at] + scale * c

    u3.wait_recv()
    for b in range(8):
        k = jnp.int32(0)
        for q in range(8):
            k = jnp.where(order[q] == b, q, k)
        for q in range(8):
            uo[0, :, 1024 * b + 128 * q:1024 * b + 128 * q + 128] = ub[k % 2, (q % 2) * 4 + k // 2, q // 2]

    for c in sent:
        c.wait_send()


def body(acts, rank_space_gradient, running_factor_blocks, inverse_root_blocks, owner_block_order, refresh):
    tokens_here = acts.shape[1]
    tokens = tokens_here * lax.axis_size("dp")
    hbm = pl.BlockSpec(memory_space=pl.ANY)
    smem = pl.BlockSpec(memory_space=pltpu.SMEM)
    vmem = pl.BlockSpec(memory_space=pltpu.VMEM)
    both, update = pl.pallas_call(
        functools.partial(kernel, tokens),
        out_shape=(
            jax.ShapeDtypeStruct((2, 32, 1024), F32),
            jax.ShapeDtypeStruct((1, 16, D), F32),
        ),
        in_specs=[smem, smem, hbm, hbm, hbm, hbm],
        out_specs=(vmem, vmem),
        scratch_shapes=[
            pltpu.VMEM((tokens_here, 1024), BF16),
            pltpu.VMEM((16, tokens_here), BF16),
            pltpu.VMEM((32, 1024), F32),
            pltpu.VMEM((4, 2, 4, 32, 1024), F32),
            pltpu.VMEM((1024, 1024), BF16),
            pltpu.VMEM((1024, 1024), BF16),
            pltpu.VMEM((64, 1536), BF16),
            pltpu.VMEM((8, 128, 640), F32),
            pltpu.VMEM((8, 2, 16, 640), F32),
            pltpu.VMEM((8, 2, 32, 640), F32),
            pltpu.VMEM((8, 2, 32, 640), F32),
            pltpu.VMEM((8, 32, 640), F32),
            pltpu.VMEM((8, 3, 8, 640), F32),
            pltpu.VMEM((8, 32, 640), F32),
            pltpu.VMEM((8, 32, 640), F32),
            pltpu.VMEM((2, 32, 640), F32),
            pltpu.VMEM((2, 32, 640), F32),
            pltpu.VMEM((8, 128, 640), F32),
            pltpu.VMEM((4, 8, 32, 128), F32),
            pltpu.VMEM((8, 32, 128), F32),
            pltpu.VMEM((8, 32, 128), F32),
            pltpu.VMEM((32, 1024), F32),
            pltpu.VMEM((128, 128), F32),
            pltpu.VMEM((2, 8, 4, 16, 128), F32),
            pltpu.SemaphoreType.DMA((8,)),
            pltpu.SemaphoreType.DMA((SEMS,)),
            pltpu.SemaphoreType.DMA((SEMS,)),
        ],
        compiler_params=pltpu.CompilerParams(
            collective_id=0, has_side_effects=True, vmem_limit_bytes=56 * 1024 * 1024
        ),
        cost_estimate=pl.CostEstimate(flops=8_000_000_000, bytes_accessed=12_000_000, transcendentals=0),
        name="kfac_step",
    )(
        owner_block_order,
        refresh,
        acts,
        jnp.swapaxes(rank_space_gradient[0], 0, 1),
        running_factor_blocks,
        inverse_root_blocks,
    )
    return both[0:1], both[1:2], update


def solution(mesh):
    return jax.shard_map(
        body,
        mesh=mesh,
        in_specs=(
            P(None, "dp", "mp"),
            P(None, "dp", None),
            P("mp", "dp", None),
            P("mp", "dp", None),
            P(),
            P(),
        ),
        out_specs=(P("mp", "dp", None), P("mp", "dp", None), P()),
        check_vma=False,
    )
```

```python
import functools

import jax
import jax.numpy as jnp
from jax import lax
from jax.experimental import pallas as pl
from jax.experimental.pallas import tpu as pltpu
from jax.sharding import PartitionSpec as P

D = 8192
DECAY = 0.75
DAMPING = 0.1
MESH = pl.DeviceIdType.MESH
NN = (((1,), (0,)), ((), ()))
NT = (((1,), (1,)), ((), ()))
TN = (((0,), (0,)), ((), ()))
SEMS = 200
F32 = jnp.float32
BF16 = jnp.bfloat16

GROUPS = ((4, 5, 6, 7), (0, 1, 2, 3))


def width(p):
    return 640 if p <= 4 else 512


def dot(a, b, dims=NN):
    return lax.dot_general(a, b, dims, preferred_element_type=F32)


def split(v):
    high = v.astype(BF16)
    return high, (v - high.astype(F32)).astype(BF16)


def dot_split(stacked, high, low, dims=NN):
    rows = stacked.shape[0] // 2
    both = dot(stacked, high, dims)
    return both[:rows] + both[rows:] + dot(stacked[:rows], low, dims)


def kernel(
    tokens,
    order, refresh, x_hbm, g_hbm, r_hbm, y_hbm,
    both, uo,
    x, g, rsh, yb, yh, yl, ystk, pan, r0, t1, r1, s1, r2, zb0, zb1, sibs, sibr, cag,
    rcol, vs, vr, f, tb, ub, lsem, ssem, rsem,
):
    scale = (1.0 - DECAY) / tokens
    zb = (zb0, zb1)
    dp = lax.axis_index("dp")
    mp = lax.axis_index("mp")
    cy, czh, cx = dp // 8, (dp // 4) % 2, dp % 4
    czl, cc = mp // 2, mp % 2
    cz = czh * 4 + czl

    def dev(y, zh, xx, zl, c):
        return {"dp": (y * 2 + zh) * 4 + xx, "mp": zl * 2 + c}

    def zdev(d):
        w = (cz + d) % 8
        return dev(cy, w // 4, cx, w % 4, cc)

    px = {d: dev(cy, czh, (cx + d) % 4, czl, cc) for d in (1, 2, 3)}
    py = {d: dev((cy + d) % 4, czh, cx, czl, cc) for d in (1, 2, 3)}
    pa = {
        (dz, dx): dev(cy, (czh + dz) % 2, (cx + dx) % 4, czl, cc)
        for dz in (0, 1) for dx in (0, 1, 2, 3) if dz or dx
    }
    pz = {d: zdev(d) for d in range(1, 8)}
    z_up, z_down = pz[1], pz[7]
    sibling = dev(cy, czh, cx, czl, 1 - cc)
    AX = {"x": (cx, px), "y": (cy, py)}

    count = [0]
    sent = []

    def send(src, dst, target):
        i = count[0]
        count[0] += 1
        copy = pltpu.make_async_remote_copy(
            src_ref=src, dst_ref=dst, send_sem=ssem.at[i], recv_sem=rsem.at[i],
            device_id=target, device_id_type=MESH,
        )
        copy.start()
        sent.append(copy)
        return copy

    def arrive(copies):
        for c in copies:
            c.wait_recv()

    own_y = yb.at[cy, czh, cx]
    load_y = pltpu.make_async_copy(y_hbm.at[0], own_y, lsem.at[0])
    load_r = pltpu.make_async_copy(r_hbm.at[0], rsh, lsem.at[1])
    load_y.start()
    load_r.start()
    nk = 4
    depth = x.shape[0] // nk
    load_x = [
        pltpu.make_async_copy(x_hbm.at[0, pl.ds(i * depth, depth)], x.at[pl.ds(i * depth, depth)], lsem.at[3 + i])
        for i in range(nk)
    ]
    for c in load_x:
        c.start()
    load_g = pltpu.make_async_copy(g_hbm, g, lsem.at[2])
    load_g.start()

    barrier = pltpu.get_barrier_semaphore()
    peers = list(pa.values()) + list(py.values()) + [pz[d] for d in (1, 2, 3, 5, 6, 7)] + [sibling]
    for peer in peers:
        pl.semaphore_signal(barrier, inc=1, device_id=peer, device_id_type=MESH)
    pl.semaphore_wait(barrier, len(peers))

    def y_first(h):
        a = [send(yb.at[cy, h, cx, pl.ds(0, 16)], yb.at[cy, h, cx, pl.ds(0, 16)], px[d]) for d in (1, 2, 3)]
        b = [send(yb.at[cy, h, cx, pl.ds(16, 16)], yb.at[cy, h, cx, pl.ds(16, 16)], py[d]) for d in (1, 2, 3)]
        return a + b

    def y_second(h):
        a = [send(yb.at[cy, h, :, pl.ds(0, 16)], yb.at[cy, h, :, pl.ds(0, 16)], py[d]) for d in (1, 3)]
        b = [send(yb.at[:, h, cx, pl.ds(16, 16)], yb.at[:, h, cx, pl.ds(16, 16)], px[d]) for d in (1, 3)]
        return a + b

    def y_third(h, copies):
        arrive(copies)
        out = []
        for d, at in ((3, 0), (1, 8)):
            ya, xa = (cy + d) % 4, (cx + d) % 4
            ref = yb.at[ya, h, :, pl.ds(at, 8)]
            out.append(send(ref, ref, py[4 - d]))
            ref = yb.at[:, h, xa, pl.ds(16 + at, 8)]
            out.append(send(ref, ref, px[4 - d]))
        return out

    my_j = czh * 4 + cx
    load_y.wait()
    y_z = send(own_y, own_y, pa[(1, 0)])
    y_own1 = y_first(czh)
    load_r.wait()
    r_a2a = []
    for (dz, dx), peer in pa.items():
        j = ((czh + dz) % 2) * 4 + (cx + dx) % 4
        r_a2a.append(
            send(rsh.at[:, pl.ds(pl.multiple_of(j * 128, 128), 128)], rcol.at[cy, my_j], peer)
        )
    rcol[cy, my_j] = rsh[:, pl.ds(pl.multiple_of(my_j * 128, 128), 128)]

    yr = yb[cy, czh, cx]
    yrh, yrl = split(yr)
    ystk[0:32, 0:1024] = yrh
    ystk[0:32, 1024:1536] = yrh[:, :512]
    ystk[32:64, 0:1024] = yrl
    ystk[32:64, 1024:1536] = yrl[:, :512]

    def gemm(i, k0, kn, first):
        lo = 256 * i
        n = 768 if i < 2 else 640
        segs = [(lo, n, 0)] if lo + n <= 1024 else [(lo, 1024 - lo, 0), (0, lo + n - 1024, 1024 - lo)]
        for start, w, at in segs:
            v = dot(x[k0:k0 + kn, lo:lo + 256], x[k0:k0 + kn, start:start + w], TN)
            for half in (0, 1):
                p = 2 * i + half
                cols = 640 if p < 4 else 512
                b0, b1 = max(at, 128 * half), min(at + w, 128 * half + cols)
                if b1 <= b0:
                    continue
                part = v[128 * half:128 * half + 128, b0 - at:b1 - at]
                c0 = b0 - 128 * half
                if first:
                    pan[p, :, c0:c0 + b1 - b0] = part
                else:
                    pan[p, :, c0:c0 + b1 - b0] += part

    ax1 = {p: AX["x" if p % 2 == 0 else "y"] for p in range(8)}
    ax2 = {p: AX["y" if p % 2 == 0 else "x"] for p in range(8)}

    def quarter(a, at=0, rows=32):
        return pl.ds(pl.multiple_of((a % 4) * 32 + at, 8), rows)

    def rs_first(p):
        a, peer = ax1[p]
        w = pl.ds(0, width(p))
        return [
            send(pan.at[p, quarter(a + 2, 16 * i, 16), w], r0.at[p, i, :, w], peer[d]) for i, d in ((0, 1), (1, 3))
        ]

    def rs_mid(p, copies):
        arrive(copies)
        a, peer = ax1[p]
        w = width(p)
        out = []
        for i, d in ((0, 1), (1, 3)):
            t1[p, i, 16 * i:16 * i + 16, :w] = pan[p, quarter(a + d, 16 * i, 16), :w] + r0[p, i, :, :w]
            t1[p, i, 16 - 16 * i:32 - 16 * i, :w] = pan[p, quarter(a + d, 16 - 16 * i, 16), :w]
            out.append(send(t1.at[p, i, :, pl.ds(0, w)], r1.at[p, i, :, pl.ds(0, w)], peer[d]))
        return out

    def rs_second(p, copies):
        arrive(copies)
        a, _ = ax1[p]
        b, peer = ax2[p]
        w = width(p)
        s1[p, :, :w] = pan[p, quarter(a), :w] + r1[p, 0, :, :w] + r1[p, 1, :, :w]
        return [
            send(
                s1.at[p, pl.ds(pl.multiple_of(((b + d) % 4) * 8, 8), 8), pl.ds(0, w)],
                r2.at[p, d - 1, :, pl.ds(0, w)], peer[d],
            )
            for d in (1, 2, 3)
        ]

    def rs_end(p, copies):
        arrive(copies)
        b, _ = ax2[p]
        w = width(p)
        gi = 0 if p >= 4 else 1
        i = p % 4
        zb[gi][cz, 8 * i:8 * i + 8, :w] = (
            s1[p, pl.ds(pl.multiple_of(b * 8, 8), 8), :w] + r2[p, 0, :, :w] + r2[p, 1, :, :w] + r2[p, 2, :, :w]
        )
        if w < 640:
            zb[gi][cz, 8 * i:8 * i + 8, w:640] = jnp.zeros((8, 640 - w), F32)

    def z_step(gi, s):
        up, down = (cz - s) % 8, (cz + s) % 8
        if s < 3:
            u, v = zb[gi].at[up], zb[gi].at[down]
        else:
            u, v = zb[gi].at[up, pl.ds(0, 16)], zb[gi].at[down, pl.ds(16, 16)]
        return [send(u, u, z_up), send(v, v, z_down)]

    b_mine = order[2 * czl + cc]
    b_other = order[2 * czl + 1 - cc]

    def picked(gi, b):
        return zb[gi][b // 2] + zb[gi][b // 2 + 4]

    def to_sibling(gi):
        sibs[gi] = jnp.where(b_other % 2 == cc, picked(gi, b_other), 0.0)
        return [send(sibs.at[gi], sibr.at[gi], sibling)]

    def take(gi):
        v = jnp.where(b_mine % 2 == cc, picked(gi, b_mine), sibr[gi])
        for i, p in enumerate(GROUPS[gi]):
            a, _ = ax1[p]
            b, _ = ax2[p]
            w = width(p)
            cag[p, pl.ds(pl.multiple_of(a * 32 + b * 8, 8), 8), :w] = v[8 * i:8 * i + 8, :w]

    def ag_first(p):
        a, _ = ax1[p]
        b, peer = ax2[p]
        ref = cag.at[p, pl.ds(pl.multiple_of(a * 32 + b * 8, 8), 8), pl.ds(0, width(p))]
        return [send(ref, ref, peer[d]) for d in (1, 2, 3)]

    def ag_second(p, copies):
        arrive(copies)
        a, peer = ax1[p]
        ref = cag.at[p, quarter(a), pl.ds(0, width(p))]
        return [send(ref, ref, peer[d]) for d in (1, 3)]

    def ag_third(p, copies):
        arrive(copies)
        a, peer = ax1[p]
        out = []
        for d, at in ((3, 0), (1, 16)):
            ref = cag.at[p, quarter(a + d, at, 16), pl.ds(0, width(p))]
            out.append(send(ref, ref, peer[4 - d]))
        return out

    c1, cm, c2, g1, g2, g3 = {}, {}, {}, {}, {}, {}
    ga, gb = GROUPS
    for k in range(nk):
        load_x[k].wait()
        gemm(2, k * depth, depth, k == 0)
    load_g.wait()
    grads = dot(g[...], x[...])
    for j in range(8):
        pan[4, 16 * j:16 * j + 16, 512:640] = grads[:, 128 * j:128 * j + 128]
    for p in (4, 5):
        c1[p] = rs_first(p)
    gemm(3, 0, x.shape[0], True)
    for p in (6, 7):
        c1[p] = rs_first(p)
    for p in (4, 5):
        cm[p] = rs_mid(p, c1[p])
    y_z.wait_recv()
    y_oth1 = y_first(1 - czh)
    gemm(0, 0, x.shape[0], True)
    for p in (0, 1):
        c1[p] = rs_first(p)
    for p in (6, 7):
        cm[p] = rs_mid(p, c1[p])
    for p in (4, 5):
        c2[p] = rs_second(p, cm[p])
    gemm(1, 0, x.shape[0], True)
    for p in (2, 3):
        c1[p] = rs_first(p)
    for p in (0, 1):
        cm[p] = rs_mid(p, c1[p])
    for p in (6, 7):
        c2[p] = rs_second(p, cm[p])
    for p in ga:
        rs_end(p, c2[p])
    za = z_step(0, 0)
    for p in (2, 3):
        cm[p] = rs_mid(p, c1[p])
    arrive(r_a2a)
    r_y = [send(rcol.at[cy], rcol.at[cy], py[d]) for d in (1, 2, 3)]
    arrive(y_own1)
    y_own2 = y_second(czh)
    arrive(za)
    za = z_step(0, 1)
    for p in (0, 1):
        c2[p] = rs_second(p, cm[p])
    arrive(za)
    za = z_step(0, 2)
    for p in (2, 3):
        c2[p] = rs_second(p, cm[p])
    for p in gb:
        rs_end(p, c2[p])
    zc = z_step(1, 0)
    arrive(za)
    za = z_step(0, 3)
    y_own3 = y_third(czh, y_own2)
    arrive(y_oth1)
    y_oth2 = y_second(1 - czh)
    arrive(zc)
    zc = z_step(1, 1)
    arrive(za)
    sa = to_sibling(0)
    arrive(zc)
    zc = z_step(1, 2)
    arrive(sa)
    take(0)
    for p in ga:
        g1[p] = ag_first(p)
    arrive(zc)
    zc = z_step(1, 3)
    for p in ga:
        g2[p] = ag_second(p, g1[p])
    arrive(zc)
    sb = to_sibling(1)
    for p in ga:
        g3[p] = ag_third(p, g2[p])
    arrive(sb)
    take(1)
    for p in gb:
        g1[p] = ag_first(p)
    y_oth3 = y_third(1 - czh, y_oth2)
    for p in gb:
        g2[p] = ag_second(p, g1[p])

    arrive(y_own3)
    arrive(g3[4])
    gk = jnp.concatenate([cag[4, 16 * j:16 * j + 16, 512:640] for j in range(8)], axis=1)
    gh, gl = split(gk)
    ph, plow = split(yb[cy, czh].reshape(128, 1024))
    cond = dot_split(jnp.concatenate([gh, gl], axis=0), ph, plow, NT)
    ub[cc, cz, cy] = cond
    u1 = [send(ub.at[cc, cz, cy], ub.at[cc, cz, cy], pz[d]) for d in range(1, 8)]

    def accumulate(p):
        nb = 5 if p < 4 else 4
        ch, cl = split(cag[p, :, :128 * nb] * scale)
        out = dot_split(ystk[:, 128 * p:128 * p + 128], ch, cl)
        for o in range(nb):
            j = (p + o) % 8
            f[:, 128 * j:128 * j + 128] += out[:, 128 * o:128 * o + 128]
        f[:, 128 * p:128 * p + 128] += dot_split(
            ystk[:, 128 * (p + 1):128 * (p + nb)], ch[:, 128:], cl[:, 128:], NT
        )

    f[...] = jnp.zeros_like(f)
    accumulate(4)
    for p in (5, 6, 7):
        arrive(g3[p])
        accumulate(p)
    arrive(u1)
    u2 = [send(ub.at[cc, :, cy], ub.at[cc, :, cy], py[d]) for d in (1, 2, 3)]
    for p in gb:
        g3[p] = ag_third(p, g2[p])

    arrive(y_oth3)

    def convert(i, carry):
        v = yb[i // 8, (i // 4) % 2, i % 4]
        h, l = split(v)
        at = pl.ds(pl.multiple_of(i * 32, 32), 32)
        yh[at] = h
        yl[at] = l
        return carry

    lax.fori_loop(0, 32, convert, 0)
    arrive(r_y)
    n = 1024
    eye = (
        lax.broadcasted_iota(jnp.int32, (n, 128), 0) == lax.broadcasted_iota(jnp.int32, (n, 128), 1) + my_j * 128
    )
    rh, rl = split(DECAY * rcol[...].reshape(n, 128) + jnp.where(eye, DAMPING, 0.0))
    rows_i = pl.ds(pl.multiple_of(cy * 256, 256), 256)
    v = dot(yh[rows_i], rh) + dot(yl[rows_i], rh) + dot(yh[rows_i], rl)
    vs[...] = v.reshape(8, 32, 128)
    v_a2a = []
    for (dz, dx), peer in pa.items():
        j = ((czh + dz) % 2) * 4 + (cx + dx) % 4
        v_a2a.append(send(vs.at[j], vr.at[my_j], peer))
    vr[my_j] = vs[my_j]

    arrive(u2)
    u3 = send(ub.at[cc], ub.at[cc], sibling)
    for p in gb:
        arrive(g3[p])
        accumulate(p)
    arrive(v_a2a)
    for j in range(8):
        f[:, 128 * j:128 * j + 128] += vr[j]

    def times_root(m):
        mh, ml = split(m)
        return dot_split(jnp.concatenate([mh, ml], axis=0), yh[...], yl[...])

    third = times_root(times_root(f[...]))
    yr = yb[cy, czh, cx]
    both[1] = jnp.where(refresh[b_mine] == 1, 1.5 * yr - 0.5 * third, yr)

    panel = 2 * cy + czh
    rows_x = pl.ds(pl.multiple_of(cx * 32, 32), 32)

    def turned(block):
        tb[...] = block.T
        return tb[rows_x, :]

    for o in range(8):
        j = (panel + o) % 8
        if o < 4:
            c = cag[panel, rows_x, 128 * o:128 * o + 128]
        elif o == 4:
            q = panel % 4
            c = jnp.where(panel < 4, cag[q, rows_x, 512:640], turned(cag[q, :, 512:640]))
        else:
            c = turned(cag[j, :, 128 * (8 - o):128 * (8 - o) + 128])
        at = pl.ds(pl.multiple_of(j * 128, 128), 128)
        both[0, :, at] = DECAY * rsh[:, at] + scale * c

    u3.wait_recv()
    for b in range(8):
        k = jnp.int32(0)
        for q in range(8):
            k = jnp.where(order[q] == b, q, k)
        for q in range(8):
            uo[0, :, 1024 * b + 128 * q:1024 * b + 128 * q + 128] = ub[k % 2, (q % 2) * 4 + k // 2, q // 2]

    for c in sent:
        c.wait_send()


def body(acts, rank_space_gradient, running_factor_blocks, inverse_root_blocks, owner_block_order, refresh):
    tokens_here = acts.shape[1]
    tokens = tokens_here * lax.axis_size("dp")
    hbm = pl.BlockSpec(memory_space=pl.ANY)
    smem = pl.BlockSpec(memory_space=pltpu.SMEM)
    vmem = pl.BlockSpec(memory_space=pltpu.VMEM)
    both, update = pl.pallas_call(
        functools.partial(kernel, tokens),
        out_shape=(
            jax.ShapeDtypeStruct((2, 32, 1024), F32),
            jax.ShapeDtypeStruct((1, 16, D), F32),
        ),
        in_specs=[smem, smem, hbm, hbm, hbm, hbm],
        out_specs=(vmem, vmem),
        scratch_shapes=[
            pltpu.VMEM((tokens_here, 1024), BF16),
            pltpu.VMEM((16, tokens_here), BF16),
            pltpu.VMEM((32, 1024), F32),
            pltpu.VMEM((4, 2, 4, 32, 1024), F32),
            pltpu.VMEM((1024, 1024), BF16),
            pltpu.VMEM((1024, 1024), BF16),
            pltpu.VMEM((64, 1536), BF16),
            pltpu.VMEM((8, 128, 640), F32),
            pltpu.VMEM((8, 2, 16, 640), F32),
            pltpu.VMEM((8, 2, 32, 640), F32),
            pltpu.VMEM((8, 2, 32, 640), F32),
            pltpu.VMEM((8, 32, 640), F32),
            pltpu.VMEM((8, 3, 8, 640), F32),
            pltpu.VMEM((8, 32, 640), F32),
            pltpu.VMEM((8, 32, 640), F32),
            pltpu.VMEM((2, 32, 640), F32),
            pltpu.VMEM((2, 32, 640), F32),
            pltpu.VMEM((8, 128, 640), F32),
            pltpu.VMEM((4, 8, 32, 128), F32),
            pltpu.VMEM((8, 32, 128), F32),
            pltpu.VMEM((8, 32, 128), F32),
            pltpu.VMEM((32, 1024), F32),
            pltpu.VMEM((128, 128), F32),
            pltpu.VMEM((2, 8, 4, 16, 128), F32),
            pltpu.SemaphoreType.DMA((8,)),
            pltpu.SemaphoreType.DMA((SEMS,)),
            pltpu.SemaphoreType.DMA((SEMS,)),
        ],
        compiler_params=pltpu.CompilerParams(
            collective_id=0, has_side_effects=True, vmem_limit_bytes=56 * 1024 * 1024
        ),
        cost_estimate=pl.CostEstimate(flops=8_000_000_000, bytes_accessed=12_000_000, transcendentals=0),
        name="kfac_step",
    )(
        owner_block_order,
        refresh,
        acts,
        jnp.swapaxes(rank_space_gradient[0], 0, 1),
        running_factor_blocks,
        inverse_root_blocks,
    )
    return both[0:1], both[1:2], update


def solution(mesh):
    return jax.shard_map(
        body,
        mesh=mesh,
        in_specs=(
            P(None, "dp", "mp"),
            P(None, "dp", None),
            P("mp", "dp", None),
            P("mp", "dp", None),
            P(),
            P(),
        ),
        out_specs=(P("mp", "dp", None), P("mp", "dp", None), P()),
        check_vma=False,
    )
```
